32 devices in a mesh: row: 2 (over x), col: 4 (over y, core), rep: 4 (over z).
Axes of the slice: x: 2, y: 2, z: 4, core: 2. Of those that a mesh axis runs over, the one named last changes fastest.
Arguments:
- integrals: bfloat16 [8, 4, 60, 128, 128], P(None, 'row', 'rep', 'col'), may hold values from -0.0625 to 0.0625
- amplitudes: bfloat16 [8, 16, 60, 128, 128], P(None, 'col', 'rep', 'row'), may hold values from -6 to 6
- virt_count: int32 [8], replicated, may hold values from 76 to 128, as said below
- occ_irrep: int32 [60], replicated, may hold values from 0 to 7
Outputs:
- cycle: bfloat16 [8, 4, 128, 16, 128], P('rep', 'row', None, 'col')
The draws below stay inside these ranges and needn't reach their ends.
Inputs may be any that keep to these rules, and one draw needn't show every extreme that they name: `virt_count`: one irrep has exactly 128 virtual orbitals.
All inputs are finite; a program needn't handle non-finite values.
Results may differ from the reference program's by a relative error of at most 0.001.
Values may be sent and summed in bfloat16 or wider, within the bound.
A program may use at most 128 MiB of HBM per device.

```python
import jax
import jax.numpy as jnp
from jax import lax

NG = 8
NVG = 128
NOCC = 60
OI = 4
OJ = 16


def draw_virt_count(key, part):
    lowest = NVG * 3 // 5
    counts = jax.random.randint(key, (NG,), lowest, NVG + 1)
    chosen = jax.random.randint(jax.random.fold_in(key, 7), (), 0, NG)
    return jnp.where(jnp.arange(NG) == chosen, NVG, counts).astype(jnp.int32)


def plant(result, own_key, least, high):
    spot = [jax.random.randint(jax.random.fold_in(own_key, axis), (), 0, length) for axis, length in enumerate(result.shape)]
    widest = result.shape.index(max(result.shape))
    beside = spot[:widest] + [(spot[widest] + 1) % result.shape[widest]] + spot[widest + 1:]
    return result.at[tuple(spot)].set(least).at[tuple(beside)].set(high)


def levels(rng, extent, shards, least, top_value):
    def one(axis_at, shards_of):
        draws = jax.random.uniform(jax.random.fold_in(jax.random.fold_in(rng, 6), axis_at), (shards_of,), jnp.float32, least / len(shards), top_value / len(shards))
        return jnp.repeat(jnp.exp(draws), extent[axis_at] // shards_of).reshape((-1,) + (1,) * (len(extent) - axis_at - 1))

    loudness = one(*shards[0])
    for cut in shards[1:]:
        loudness = loudness * one(*cut)
    return loudness


def bell_draw(key, extent, spread, most, pieces=(), held_as=jnp.bfloat16):
    values = jax.random.normal(key, extent, jnp.float32) * spread
    if len(pieces) > 0:
        values = levels(key, extent, pieces, -0.22, 0.18) * values
    return jnp.clip(values, min=-most, max=most).astype(held_as)


def setup_inputs(seed: int = 0) -> dict:
    seeds = jax.random.split(jax.random.key(seed), 5)
    return {
        "integrals": bell_draw(seeds[0], (NG, OI, NOCC, NVG, NVG), (NOCC * NVG) ** -0.5, 0.0625, ((1, 2), (2, 4), (3, 4))),
        "amplitudes": bell_draw(seeds[1], (NG, OJ, NOCC, NVG, NVG), 1.0, 6.0, ((1, 4), (2, 4), (3, 2))),
        "virt_count": draw_virt_count(jax.random.fold_in(seeds[4], 71), 0),
        "occ_irrep": plant(jax.random.randint(seeds[3], (NOCC,), 0, 8), jax.random.fold_in(seeds[3], 1), 0, 7).astype(jnp.int32),
    }


def reference(integrals, amplitudes, virt_count, occ_irrep):
    groups = jnp.arange(NG, dtype=jnp.int32)
    blocks = jnp.bitwise_xor(groups[:, None], occ_irrep[None, :].astype(jnp.int32))
    limit = virt_count[blocks]
    places = jnp.arange(NVG, dtype=jnp.int32)
    c_mask = places[None, None, :] < limit[:, :, None]
    a_mask = places[None, :] < virt_count[:, None]

    def one_block(items):
        weights, amps, alive, c_live = items
        keep = c_live[:, :, None] & alive[None, None, :]
        masked = jnp.where(keep[None], weights, jnp.zeros_like(weights))
        left = masked.astype(jnp.float32)
        right = amps.astype(jnp.float32)
        product = jnp.einsum("ikca,jkcb->iajb", left, right, precision=lax.Precision.HIGHEST)
        product = jnp.where(alive[None, None, None, :], product, jnp.zeros_like(product))
        return product.astype(jnp.bfloat16)

    return lax.map(one_block, (integrals, amplitudes, a_mask, c_mask))
```

```python
import functools

import jax
import jax.numpy as jnp
from jax import lax
from jax.experimental import pallas as pl
from jax.experimental.pallas import tpu as pltpu
from jax.sharding import PartitionSpec as P

MESH = pl.DeviceIdType.MESH
TOP = 32767.0
PAD = 16


def contract(w_part, t_part):
    w_full = lax.all_gather(w_part, "col", axis=3, tiled=True)
    return jnp.einsum(
        "gikca,gjkcb->giajb",
        w_full,
        lax.all_gather(t_part, "row", axis=3, tiled=True),
        preferred_element_type=jnp.float32,
    )


def quantise(value, ref):
    rows = value.shape[0]
    most = jnp.max(jnp.abs(value), axis=0, keepdims=True)
    code = jnp.ceil(8.0 * jnp.log2(jnp.maximum(most, 1e-30)))
    scaled = jnp.clip(jnp.round(value * (jnp.exp2(code * -0.125) * TOP)), -TOP, TOP)
    ref[0:rows, :] = scaled.astype(jnp.int32).astype(jnp.int16)
    wide = jnp.broadcast_to(code, (PAD, value.shape[1]))
    ref[rows : rows + PAD, :] = wide.astype(jnp.int32).astype(jnp.int16)


def dequantise(ref):
    rows = ref.shape[0] - PAD
    code = ref[rows : rows + PAD, :].astype(jnp.int32).astype(jnp.float32)[0:1, :]
    return ref[0:rows, :].astype(jnp.int32).astype(jnp.float32) * (jnp.exp2(code * 0.125) * (1.0 / TOP))


def kernel(nz, w_ref, t_ref, o_ref, wv, tv, st, pown, xs, xr, zs, zr,
           t_sem, l_sem, s1, s2, sc, sx, sz, r_own, r_oth, r_st, r_c, r_x, r_z):
    ng, nk, cw, m = w_ref.shape
    nj, nb = t_ref.shape[1], t_ref.shape[4]
    n = nj * nb
    depth = nk * 2 * cw
    gz = ng // nz
    x, col, z = lax.axis_index("row"), lax.axis_index("col"), lax.axis_index("rep")
    y, core = col // 2, col % 2
    xn = (1 - x, col, z)
    yn = (x, (1 - y) * 2 + core, z)
    sib = (x, y * 2 + 1 - core, z)
    home = x == y
    away = x != y
    crow = pl.ds(pl.multiple_of(core * cw, cw), cw)
    crow_sib = pl.ds(pl.multiple_of((1 - core) * cw, cw), cw)
    own = pl.ds(pl.multiple_of(x * m, m), m)
    oth = pl.ds(pl.multiple_of((1 - x) * m, m), m)

    def group(t):
        return lax.rem(z + 1 + t // gz, nz) * gz + lax.rem(t, gz)

    def remote(src, dst, send, recv, dev):
        return pltpu.make_async_remote_copy(
            src_ref=src, dst_ref=dst, send_sem=send, recv_sem=recv, device_id=dev, device_id_type=MESH
        )

    def wait_oth(g):
        remote(wv.at[g, :, crow, oth], wv.at[g, :, crow, oth], s2.at[g], r_oth.at[g], xn).wait_recv()

    barrier = pltpu.get_barrier_semaphore()
    others = [xn, yn, sib] + [(x, col, lax.rem(z + d, nz)) for d in range(1, nz)]
    for dev in others:
        pl.semaphore_signal(barrier, inc=1, device_id=dev, device_id_type=MESH)
    pl.semaphore_wait(barrier, len(others))

    def begin(t, carry):
        g = group(t)
        even = lax.rem(t, 2) == 0

        @pl.when(home)
        def _():
            remote(w_ref.at[g], wv.at[g, :, crow, own], s1.at[g], r_own.at[g], yn).start()
            pltpu.make_async_copy(w_ref.at[g], wv.at[g, :, crow, own], l_sem.at[g]).start()

        @pl.when(jnp.logical_and(away, even))
        def _():
            remote(w_ref.at[g], wv.at[g, :, crow, own], s1.at[g], r_oth.at[g], xn).start()

        @pl.when(jnp.logical_and(away, jnp.logical_not(even)))
        def _():
            remote(w_ref.at[g], st.at[g], s1.at[g], r_st.at[g], yn).start()

        for j in range(nj):
            pltpu.make_async_copy(
                t_ref.at[g, j], tv.at[g, :, :, pl.ds(j * nb, nb)], t_sem.at[g, j]
            ).start()
        return carry

    lax.fori_loop(0, ng, begin, 0)

    def forward(t):
        g = group(t)
        even = lax.rem(t, 2) == 0

        @pl.when(jnp.logical_and(home, jnp.logical_not(even)))
        def _():
            remote(st.at[g], st.at[g], s1.at[g], r_st.at[g], yn).wait_recv()
            remote(st.at[g], wv.at[g, :, crow, own], s2.at[g], r_oth.at[g], xn).start()

        @pl.when(home == even)
        def _():
            wait_oth(g)
            remote(wv.at[g, :, crow, oth], wv.at[g, :, crow, oth], s2.at[g], r_oth.at[g], yn).start()

    def share(t):
        g = group(t)
        even = lax.rem(t, 2) == 0

        @pl.when(home != even)
        def _():
            wait_oth(g)

        @pl.when(home)
        def _():
            pltpu.make_async_copy(w_ref.at[g], wv.at[g, :, crow, own], l_sem.at[g]).wait()

        @pl.when(away)
        def _():
            remote(w_ref.at[g], wv.at[g, :, crow, own], s1.at[g], r_own.at[g], yn).wait_recv()

        remote(wv.at[g, :, crow, :], wv.at[g, :, crow, :], sc.at[g], r_c.at[g], sib).start()

    def product(g, lanes):
        return lax.dot_general(
            wv[g, :, :, lanes].reshape(depth, m),
            tv[g].reshape(depth, n),
            (((0,), (0,)), ((), ())),
            preferred_element_type=jnp.float32,
        )

    def multiply(t):
        g = group(t)
        for j in range(nj):
            pltpu.make_async_copy(
                t_ref.at[g, j], tv.at[g, :, :, pl.ds(j * nb, nb)], t_sem.at[g, j]
            ).wait()
        remote(wv.at[g, :, crow, :], wv.at[g, :, crow_sib, :], sc.at[g], r_c.at[g], sib).wait_recv()
        quantise(product(g, oth), xs.at[g])
        remote(xs.at[g], xr.at[g], sx.at[g], r_x.at[g], xn).start()
        pown[g] = product(g, own)

    def owner(t):
        return lax.rem(z + 1 + t // gz, nz)

    def reduce(t):
        g = group(t)
        remote(xs.at[g], xr.at[g], sx.at[g], r_x.at[g], xn).wait_recv()
        total = pown[g] + dequantise(xr.at[g])

        @pl.when(t < ng - gz)
        def _():
            quantise(total, zs.at[g])
            slot = lax.rem(t, gz)
            remote(zs.at[g], zr.at[z, slot], sz.at[g], r_z.at[z, slot], (x, col, owner(t))).start()

        @pl.when(t >= ng - gz)
        def _():
            o_ref[lax.rem(t, gz)] = total

    def step(t, carry):
        @pl.when(t < ng)
        def _():
            forward(t)

        @pl.when(jnp.logical_and(t >= 1, t < ng + 1))
        def _():
            share(t - 1)
            multiply(t - 1)

        @pl.when(t >= 2)
        def _():
            reduce(t - 2)

        return carry

    lax.fori_loop(0, ng + 2, step, 0)

    for d in range(nz - 1, 0, -1):
        src = lax.rem(z + nz - d, nz)
        for slot in range(gz):
            remote(zr.at[src, slot], zr.at[src, slot], sz.at[0], r_z.at[src, slot], xn).wait_recv()
            o_ref[slot] += dequantise(zr.at[src, slot])

    def finish(t, carry):
        g = group(t)
        even = lax.rem(t, 2) == 0
        remote(w_ref.at[g], st.at[g], s1.at[g], r_st.at[g], yn).wait_send()

        @pl.when(jnp.logical_or(home, jnp.logical_not(even)))
        def _():
            remote(st.at[g], st.at[g], s2.at[g], r_oth.at[g], xn).wait_send()

        remote(wv.at[g, :, crow, :], wv.at[g, :, crow, :], sc.at[g], r_c.at[g], sib).wait_send()
        remote(xs.at[g], xr.at[g], sx.at[g], r_x.at[g], xn).wait_send()

        @pl.when(t < ng - gz)
        def _():
            remote(zs.at[g], zs.at[g], sz.at[g], r_x.at[g], xn).wait_send()

        return carry

    lax.fori_loop(0, ng, finish, 0)


def fused(masked, amplitudes):
    ng, ni, nk, cw, na = masked.shape
    nj, nb = amplitudes.shape[1], amplitudes.shape[4]
    nz = lax.axis_size("rep")
    m, n, gz = ni * na, nj * nb, ng // nz
    w = jnp.transpose(masked, (0, 2, 3, 1, 4)).reshape(ng, nk, cw, m)
    dma = pltpu.SemaphoreType.DMA
    part = functools.partial
    coded = (m + PAD, n)
    return pl.pallas_call(
        part(kernel, nz),
        out_shape=jax.ShapeDtypeStruct((gz, m, n), jnp.float32),
        in_specs=[pl.BlockSpec(memory_space=pl.ANY)] * 2,
        out_specs=pl.BlockSpec(memory_space=pltpu.VMEM),
        scratch_shapes=[
            pltpu.VMEM((ng, nk, 2 * cw, 2 * m), jnp.bfloat16),
            pltpu.VMEM((ng, nk, 2 * cw, n), jnp.bfloat16),
            pltpu.VMEM((ng, nk, cw, m), jnp.bfloat16),
            pltpu.VMEM((ng, m, n), jnp.float32),
            pltpu.VMEM((ng,) + coded, jnp.int16),
            pltpu.VMEM((ng,) + coded, jnp.int16),
            pltpu.VMEM((ng,) + coded, jnp.int16),
            pltpu.VMEM((nz, gz) + coded, jnp.int16),
            dma((ng, nj)),
        ]
        + [dma((ng,))] * 11
        + [dma((nz, gz))],
        compiler_params=pltpu.CompilerParams(
            collective_id=0, has_side_effects=True, vmem_limit_bytes=56 * 1024 * 1024
        ),
    )(w, amplitudes)


def body(integrals, amplitudes, virt_count, occ_irrep):
    ngroup, ni, k_local, c_local, nvirt = integrals.shape
    nj = amplitudes.shape[1]
    rep_index = lax.axis_index("rep")
    col_index = lax.axis_index("col")
    occ_local = lax.dynamic_slice_in_dim(occ_irrep, rep_index * k_local, k_local)
    groups = jnp.arange(ngroup, dtype=jnp.int32)
    blocks = jnp.bitwise_xor(groups[:, None], occ_local[None, :])
    onehot = blocks[:, :, None] == groups[None, None, :]
    limit = jnp.sum(jnp.where(onehot, virt_count[None, None, :], 0), axis=2)
    c_global = col_index * c_local + jnp.arange(c_local, dtype=jnp.int32)
    c_live = c_global[None, None, :] < limit[:, :, None]
    places = jnp.arange(nvirt, dtype=jnp.int32)
    a_live = places[None, :] < virt_count[:, None]
    keep = c_live[:, None, :, :, None] & a_live[:, None, None, None, :]
    masked = jnp.where(keep, integrals, jnp.zeros_like(integrals))
    owned = ngroup // lax.axis_size("rep")
    if lax.axis_size("row") == 2 and lax.axis_size("col") == 4 and amplitudes.shape[3] == 2 * c_local:
        summed = fused(masked, amplitudes).reshape(owned, ni, nvirt, nj, nvirt)
    else:
        partial_cycle = contract(masked, amplitudes)
        summed = lax.psum_scatter(partial_cycle, "rep", scatter_dimension=0, tiled=True)
    own_counts = lax.dynamic_slice_in_dim(virt_count, rep_index * owned, owned)
    b_live = places[None, :] < own_counts[:, None]
    result = jnp.where(b_live[:, None, None, None, :], summed, jnp.zeros_like(summed))
    return result.astype(jnp.bfloat16)


def solution(mesh):
    return jax.shard_map(
        body,
        mesh=mesh,
        in_specs=(P(None, "row", "rep", "col", None), P(None, "col", "rep", "row", None), P(), P()),
        out_specs=P("rep", "row", None, "col", None),
        check_vma=False,
    )
```

```python
import functools

import jax
import jax.numpy as jnp
from jax import lax
from jax.experimental import pallas as pl
from jax.experimental.pallas import tpu as pltpu
from jax.sharding import PartitionSpec as P

MESH = pl.DeviceIdType.MESH
TOP = 32767.0
PAD = 16
AHEAD = 2


def contract(w_part, t_part):
    w_full = lax.all_gather(w_part, "col", axis=3, tiled=True)
    return jnp.einsum(
        "gikca,gjkcb->giajb",
        w_full,
        lax.all_gather(t_part, "row", axis=3, tiled=True),
        preferred_element_type=jnp.float32,
    )


def quantise(value, ref):
    rows = value.shape[0]
    most = jnp.max(jnp.abs(value), axis=0, keepdims=True)
    code = jnp.ceil(8.0 * jnp.log2(jnp.maximum(most, 1e-30)))
    scaled = jnp.clip(jnp.round(value * (jnp.exp2(code * -0.125) * TOP)), -TOP, TOP)
    ref[0:rows, :] = scaled.astype(jnp.int32).astype(jnp.int16)
    wide = jnp.broadcast_to(code, (PAD, value.shape[1]))
    ref[rows : rows + PAD, :] = wide.astype(jnp.int32).astype(jnp.int16)


def dequantise(ref):
    rows = ref.shape[0] - PAD
    code = ref[rows : rows + PAD, :].astype(jnp.int32).astype(jnp.float32)[0:1, :]
    return ref[0:rows, :].astype(jnp.int32).astype(jnp.float32) * (jnp.exp2(code * 0.125) * (1.0 / TOP))


def kernel(nz, count_ref, occ_ref, w_ref, t_ref, o_ref, wv, wm, tv, st, pown, xs, xr, zs, zr,
           t_sem, l_sem, s1, s2, sc, sx, sz, r_own, r_oth, r_st, r_c, r_x, r_z):
    ng, ni, nk, cw, na = w_ref.shape
    m = ni * na
    nj, nb = t_ref.shape[1], t_ref.shape[4]
    n = nj * nb
    depth = nk * 2 * cw
    gz = ng // nz
    x, col, z = lax.axis_index("row"), lax.axis_index("col"), lax.axis_index("rep")
    y, core = col // 2, col % 2
    xn = (1 - x, col, z)
    yn = (x, (1 - y) * 2 + core, z)
    sib = (x, y * 2 + 1 - core, z)
    home = x == y
    away = x != y
    crow = pl.ds(pl.multiple_of(core * cw, cw), cw)
    crow_sib = pl.ds(pl.multiple_of((1 - core) * cw, cw), cw)
    own = pl.ds(pl.multiple_of(x * m, m), m)
    oth = pl.ds(pl.multiple_of((1 - x) * m, m), m)

    def group(t):
        return lax.rem(z + 1 + t // gz, nz) * gz + lax.rem(t, gz)

    def remote(src, dst, send, recv, dev):
        return pltpu.make_async_remote_copy(
            src_ref=src, dst_ref=dst, send_sem=send, recv_sem=recv, device_id=dev, device_id_type=MESH
        )

    def wait_oth(g):
        remote(wv.at[g, :, crow, oth], wv.at[g, :, crow, oth], s2.at[g], r_oth.at[g], xn).wait_recv()

    barrier = pltpu.get_barrier_semaphore()
    others = [xn, yn, sib] + [(x, col, lax.rem(z + d, nz)) for d in range(1, nz)]
    for dev in others:
        pl.semaphore_signal(barrier, inc=1, device_id=dev, device_id_type=MESH)
    pl.semaphore_wait(barrier, len(others))

    def pieces(g, dst, send, recv, dev):
        for i in range(ni):
            remote(w_ref.at[g, i], dst.at[:, :, pl.ds(i * na, na)], send, recv, dev).start()

    def begin(t):
        g = group(t)
        even = lax.rem(t, 2) == 0
        mine = wv.at[g, :, crow, own]

        @pl.when(home)
        def _():
            pieces(g, mine, s1.at[g], r_own.at[g], yn)
            for i in range(ni):
                pltpu.make_async_copy(w_ref.at[g, i], mine.at[:, :, pl.ds(i * na, na)], l_sem.at[g]).start()

        @pl.when(jnp.logical_and(away, even))
        def _():
            pieces(g, mine, s1.at[g], r_oth.at[g], xn)

        @pl.when(jnp.logical_and(away, jnp.logical_not(even)))
        def _():
            pieces(g, st.at[g], s1.at[g], r_st.at[g], yn)

        for j in range(nj):
            pltpu.make_async_copy(
                t_ref.at[g, j], tv.at[g, :, :, pl.ds(j * nb, nb)], t_sem.at[g, j]
            ).start()

    for t in range(AHEAD):
        begin(t)

    def forward(t):
        g = group(t)
        even = lax.rem(t, 2) == 0

        @pl.when(jnp.logical_and(home, jnp.logical_not(even)))
        def _():
            remote(st.at[g], st.at[g], s1.at[g], r_st.at[g], yn).wait_recv()
            remote(st.at[g], wv.at[g, :, crow, own], s2.at[g], r_oth.at[g], xn).start()

        @pl.when(jnp.logical_and(home, even))
        def _():
            wait_oth(g)
            remote(wv.at[g, :, crow, oth], wv.at[g, :, crow, oth], s2.at[g], r_oth.at[g], yn).start()

    def onward(t):
        g = group(t)

        @pl.when(jnp.logical_and(away, lax.rem(t, 2) == 1))
        def _():
            wait_oth(g)
            remote(wv.at[g, :, crow, oth], wv.at[g, :, crow, oth], s2.at[g], r_oth.at[g], yn).start()

    def share(t):
        g = group(t)
        even = lax.rem(t, 2) == 0

        @pl.when(home != even)
        def _():
            wait_oth(g)

        @pl.when(home)
        def _():
            pltpu.make_async_copy(st.at[g], wv.at[g, :, crow, own], l_sem.at[g]).wait()

        @pl.when(away)
        def _():
            remote(st.at[g], wv.at[g, :, crow, own], s1.at[g], r_own.at[g], yn).wait_recv()

        remote(wv.at[g, :, crow, :], wv.at[g, :, crow, :], sc.at[g], r_c.at[g], sib).start()

    def product(g, lanes):
        return lax.dot_general(
            wm[:, :, lanes].reshape(depth, m),
            tv[g].reshape(depth, n),
            (((0,), (0,)), ((), ())),
            preferred_element_type=jnp.float32,
        )

    def multiply(t):
        g = group(t)
        for j in range(nj):
            pltpu.make_async_copy(
                t_ref.at[g, j], tv.at[g, :, :, pl.ds(j * nb, nb)], t_sem.at[g, j]
            ).wait()
        remote(wv.at[g, :, crow, :], wv.at[g, :, crow_sib, :], sc.at[g], r_c.at[g], sib).wait_recv()
        rows = x * (2 * cw) + lax.broadcasted_iota(jnp.int32, (2 * cw, 2 * m), 0)
        a_live = lax.rem(lax.broadcasted_iota(jnp.int32, (2 * cw, 2 * m), 1), na) < count_ref[g]
        for k in range(nk):
            limit = count_ref[jnp.bitwise_xor(g, occ_ref[z * nk + k])]
            keep = jnp.where(jnp.logical_and(a_live, rows < limit), 1.0, 0.0).astype(jnp.bfloat16)
            wm[k] = wv[g, k] * keep
        quantise(product(g, oth), xs.at[g])
        remote(xs.at[g], xr.at[g], sx.at[g], r_x.at[g], xn).start()
        pown[g] = product(g, own)

    def owner(t):
        return lax.rem(z + 1 + t // gz, nz)

    def reduce(t):
        g = group(t)
        remote(xs.at[g], xr.at[g], sx.at[g], r_x.at[g], xn).wait_recv()
        total = pown[g] + dequantise(xr.at[g])

        @pl.when(t < ng - gz)
        def _():
            quantise(total, zs.at[g])
            slot = lax.rem(t, gz)
            remote(zs.at[g], zr.at[z, slot], sz.at[g], r_z.at[z, slot], (x, col, owner(t))).start()

        @pl.when(t >= ng - gz)
        def _():
            o_ref[lax.rem(t, gz)] = total

    def step(t, carry):
        @pl.when(t < ng)
        def _():
            forward(t)

        @pl.when(jnp.logical_and(t >= 1, t < ng + 1))
        def _():
            onward(t - 1)

        @pl.when(t < ng - AHEAD)
        def _():
            begin(t + AHEAD)

        @pl.when(jnp.logical_and(t >= 2, t < ng + 2))
        def _():
            share(t - 2)
            multiply(t - 2)

        @pl.when(t >= 3)
        def _():
            reduce(t - 3)

        return carry

    lax.fori_loop(0, ng + 3, step, 0)

    for d in range(nz - 1, 0, -1):
        src = lax.rem(z + nz - d, nz)
        for slot in range(gz):
            remote(zr.at[src, slot], zr.at[src, slot], sz.at[0], r_z.at[src, slot], xn).wait_recv()
            o_ref[slot] += dequantise(zr.at[src, slot])

    def finish(t, carry):
        g = group(t)
        even = lax.rem(t, 2) == 0
        remote(st.at[g], st.at[g], s1.at[g], r_st.at[g], yn).wait_send()

        @pl.when(jnp.logical_or(home, jnp.logical_not(even)))
        def _():
            remote(st.at[g], st.at[g], s2.at[g], r_oth.at[g], xn).wait_send()

        remote(wv.at[g, :, crow, :], wv.at[g, :, crow, :], sc.at[g], r_c.at[g], sib).wait_send()
        remote(xs.at[g], xr.at[g], sx.at[g], r_x.at[g], xn).wait_send()

        @pl.when(t < ng - gz)
        def _():
            remote(zs.at[g], zs.at[g], sz.at[g], r_x.at[g], xn).wait_send()

        return carry

    lax.fori_loop(0, ng, finish, 0)


def fused(integrals, amplitudes, virt_count, occ_irrep):
    ng, ni, nk, cw, na = integrals.shape
    nj, nb = amplitudes.shape[1], amplitudes.shape[4]
    nz = lax.axis_size("rep")
    m, n, gz = ni * na, nj * nb, ng // nz
    dma = pltpu.SemaphoreType.DMA
    part = functools.partial
    coded = (m + PAD, n)
    return pl.pallas_call(
        part(kernel, nz),
        out_shape=jax.ShapeDtypeStruct((gz, m, n), jnp.float32),
        in_specs=[pl.BlockSpec(memory_space=pltpu.SMEM)] * 2 + [pl.BlockSpec(memory_space=pl.ANY)] * 2,
        out_specs=pl.BlockSpec(memory_space=pltpu.VMEM),
        scratch_shapes=[
            pltpu.VMEM((ng, nk, 2 * cw, 2 * m), jnp.bfloat16),
            pltpu.VMEM((nk, 2 * cw, 2 * m), jnp.bfloat16),
            pltpu.VMEM((ng, nk, 2 * cw, n), jnp.bfloat16),
            pltpu.VMEM((ng, nk, cw, m), jnp.bfloat16),
            pltpu.VMEM((ng, m, n), jnp.float32),
            pltpu.VMEM((ng,) + coded, jnp.int16),
            pltpu.VMEM((ng,) + coded, jnp.int16),
            pltpu.VMEM((ng,) + coded, jnp.int16),
            pltpu.VMEM((nz, gz) + coded, jnp.int16),
            dma((ng, nj)),
        ]
        + [dma((ng,))] * 11
        + [dma((nz, gz))],
        compiler_params=pltpu.CompilerParams(
            collective_id=0, has_side_effects=True, vmem_limit_bytes=56 * 1024 * 1024
        ),
    )(virt_count, occ_irrep, integrals, amplitudes)


def gathered(integrals, amplitudes, virt_count, occ_irrep):
    ngroup, _, k_local, c_local, nvirt = integrals.shape
    occ_local = lax.dynamic_slice_in_dim(occ_irrep, lax.axis_index("rep") * k_local, k_local)
    groups = jnp.arange(ngroup, dtype=jnp.int32)
    blocks = jnp.bitwise_xor(groups[:, None], occ_local[None, :])
    onehot = blocks[:, :, None] == groups[None, None, :]
    limit = jnp.sum(jnp.where(onehot, virt_count[None, None, :], 0), axis=2)
    c_global = lax.axis_index("col") * c_local + jnp.arange(c_local, dtype=jnp.int32)
    c_live = c_global[None, None, :] < limit[:, :, None]
    a_live = jnp.arange(nvirt, dtype=jnp.int32)[None, :] < virt_count[:, None]
    keep = c_live[:, None, :, :, None] & a_live[:, None, None, None, :]
    masked = jnp.where(keep, integrals, jnp.zeros_like(integrals))
    partial_cycle = contract(masked, amplitudes)
    return lax.psum_scatter(partial_cycle, "rep", scatter_dimension=0, tiled=True)


def body(integrals, amplitudes, virt_count, occ_irrep):
    ngroup, ni, _, c_local, nvirt = integrals.shape
    nj = amplitudes.shape[1]
    owned = ngroup // lax.axis_size("rep")
    if lax.axis_size("row") == 2 and lax.axis_size("col") == 4 and amplitudes.shape[3] == 2 * c_local:
        summed = fused(integrals, amplitudes, virt_count, occ_irrep)
        summed = summed.reshape(owned, ni, nvirt, nj, nvirt)
    else:
        summed = gathered(integrals, amplitudes, virt_count, occ_irrep)
    own_counts = lax.dynamic_slice_in_dim(virt_count, lax.axis_index("rep") * owned, owned)
    b_live = jnp.arange(nvirt, dtype=jnp.int32)[None, :] < own_counts[:, None]
    result = jnp.where(b_live[:, None, None, None, :], summed, jnp.zeros_like(summed))
    return result.astype(jnp.bfloat16)


def solution(mesh):
    return jax.shard_map(
        body,
        mesh=mesh,
        in_specs=(P(None, "row", "rep", "col", None), P(None, "col", "rep", "row", None), P(), P()),
        out_specs=P("rep", "row", None, "col", None),
        check_vma=False,
    )
```

```python
import functools

import jax
import jax.numpy as jnp
from jax import lax
from jax.experimental import pallas as pl
from jax.experimental.pallas import tpu as pltpu
from jax.sharding import PartitionSpec as P

MESH = pl.DeviceIdType.MESH
TOP = 32767.0
PAD = 16
AHEAD = 2


def contract(w_part, t_part):
    w_full = lax.all_gather(w_part, "col", axis=3, tiled=True)
    return jnp.einsum(
        "gikca,gjkcb->giajb",
        w_full,
        lax.all_gather(t_part, "row", axis=3, tiled=True),
        preferred_element_type=jnp.float32,
    )


def quantise(value, ref):
    rows = value.shape[0]
    most = jnp.max(jnp.abs(value), axis=0, keepdims=True)
    code = jnp.ceil(8.0 * jnp.log2(jnp.maximum(most, 1e-30)))
    scaled = jnp.clip(jnp.round(value * (jnp.exp2(code * -0.125) * TOP)), -TOP, TOP)
    ref[0:rows, :] = scaled.astype(jnp.int32).astype(jnp.int16)
    wide = jnp.broadcast_to(code, (PAD, value.shape[1]))
    ref[rows : rows + PAD, :] = wide.astype(jnp.int32).astype(jnp.int16)


def dequantise(ref):
    rows = ref.shape[0] - PAD
    code = ref[rows : rows + PAD, :].astype(jnp.int32).astype(jnp.float32)[0:1, :]
    return ref[0:rows, :].astype(jnp.int32).astype(jnp.float32) * (jnp.exp2(code * 0.125) * (1.0 / TOP))


def kernel(nz, count_ref, occ_ref, w_ref, t_ref, o_ref, wv, wm, tv, st, pown, xs, xr, zs, zr,
           t_sem, l_sem, s1, s2, sc, sx, sz, r_own, r_oth, r_st, r_c, r_x, r_z):
    ng, ni, nk, cw, na = w_ref.shape
    m = ni * na
    nj, nb = t_ref.shape[1], t_ref.shape[4]
    n = nj * nb
    depth = nk * 2 * cw
    gz = ng // nz
    x, col, z = lax.axis_index("row"), lax.axis_index("col"), lax.axis_index("rep")
    y, core = col // 2, col % 2
    xn = (1 - x, col, z)
    yn = (x, (1 - y) * 2 + core, z)
    sib = (x, y * 2 + 1 - core, z)
    home = x == y
    away = x != y
    crow = pl.ds(pl.multiple_of(core * cw, cw), cw)
    crow_sib = pl.ds(pl.multiple_of((1 - core) * cw, cw), cw)
    own = pl.ds(pl.multiple_of(x * m, m), m)
    oth = pl.ds(pl.multiple_of((1 - x) * m, m), m)

    def group(t):
        return lax.rem(z + 1 + t // gz, nz) * gz + lax.rem(t, gz)

    def remote(src, dst, send, recv, dev):
        return pltpu.make_async_remote_copy(
            src_ref=src, dst_ref=dst, send_sem=send, recv_sem=recv, device_id=dev, device_id_type=MESH
        )

    def wait_oth(g):
        remote(wv.at[g, :, crow, oth], wv.at[g, :, crow, oth], s2.at[g], r_oth.at[g], xn).wait_recv()

    barrier = pltpu.get_barrier_semaphore()
    others = [xn, yn, sib] + [(x, col, lax.rem(z + d, nz)) for d in range(1, nz)]
    for dev in others:
        pl.semaphore_signal(barrier, inc=1, device_id=dev, device_id_type=MESH)
    pl.semaphore_wait(barrier, len(others))

    def pieces(g, dst, send, recv, dev):
        for i in range(ni):
            remote(w_ref.at[g, i], dst.at[:, :, pl.ds(i * na, na)], send, recv, dev).start()

    def begin(t):
        g = group(t)
        even = lax.rem(t, 2) == 0
        mine = wv.at[g, :, crow, own]

        @pl.when(home)
        def _():
            pieces(g, mine, s1.at[g], r_own.at[g], yn)
            for i in range(ni):
                pltpu.make_async_copy(w_ref.at[g, i], mine.at[:, :, pl.ds(i * na, na)], l_sem.at[g]).start()

        @pl.when(jnp.logical_and(away, even))
        def _():
            pieces(g, mine, s1.at[g], r_oth.at[g], xn)

        @pl.when(jnp.logical_and(away, jnp.logical_not(even)))
        def _():
            pieces(g, st.at[g], s1.at[g], r_st.at[g], yn)

        for j in range(nj):
            pltpu.make_async_copy(
                t_ref.at[g, j], tv.at[g, :, :, pl.ds(j * nb, nb)], t_sem.at[g, j]
            ).start()

    for t in range(AHEAD):
        begin(t)

    def forward(t):
        g = group(t)
        even = lax.rem(t, 2) == 0

        @pl.when(jnp.logical_and(home, jnp.logical_not(even)))
        def _():
            remote(st.at[g], st.at[g], s1.at[g], r_st.at[g], yn).wait_recv()
            remote(st.at[g], wv.at[g, :, crow, own], s2.at[g], r_oth.at[g], xn).start()

        @pl.when(jnp.logical_and(home, even))
        def _():
            wait_oth(g)
            remote(wv.at[g, :, crow, oth], wv.at[g, :, crow, oth], s2.at[g], r_oth.at[g], yn).start()

    def onward(t):
        g = group(t)

        @pl.when(jnp.logical_and(away, lax.rem(t, 2) == 1))
        def _():
            wait_oth(g)
            remote(wv.at[g, :, crow, oth], wv.at[g, :, crow, oth], s2.at[g], r_oth.at[g], yn).start()

    def share(t):
        g = group(t)
        even = lax.rem(t, 2) == 0

        @pl.when(home != even)
        def _():
            wait_oth(g)

        @pl.when(home)
        def _():
            pltpu.make_async_copy(st.at[g], wv.at[g, :, crow, own], l_sem.at[g]).wait()

        @pl.when(away)
        def _():
            remote(st.at[g], wv.at[g, :, crow, own], s1.at[g], r_own.at[g], yn).wait_recv()

        remote(wv.at[g, :, crow, :], wv.at[g, :, crow, :], sc.at[g], r_c.at[g], sib).start()

    def product(g, lanes):
        return lax.dot_general(
            wm[:, :, lanes].reshape(depth, m),
            tv[g].reshape(depth, n),
            (((0,), (0,)), ((), ())),
            preferred_element_type=jnp.float32,
        )

    def multiply(t):
        g = group(t)
        for j in range(nj):
            pltpu.make_async_copy(
                t_ref.at[g, j], tv.at[g, :, :, pl.ds(j * nb, nb)], t_sem.at[g, j]
            ).wait()
        remote(wv.at[g, :, crow, :], wv.at[g, :, crow_sib, :], sc.at[g], r_c.at[g], sib).wait_recv()
        rows = x * (2 * cw) + lax.broadcasted_iota(jnp.int32, (2 * cw, 2 * m), 0)
        a_live = lax.rem(lax.broadcasted_iota(jnp.int32, (2 * cw, 2 * m), 1), na) < count_ref[g]
        for k in range(nk):
            limit = count_ref[jnp.bitwise_xor(g, occ_ref[z * nk + k])]
            keep = jnp.where(jnp.logical_and(a_live, rows < limit), 1.0, 0.0).astype(jnp.bfloat16)
            wm[k] = wv[g, k] * keep
        quantise(product(g, oth), xs.at[g])
        remote(xs.at[g], xr.at[g], sx.at[g], r_x.at[g], xn).start()
        pown[g] = product(g, own)

    def owner(t):
        return lax.rem(z + 1 + t // gz, nz)

    def reduce(t):
        g = group(t)
        remote(xs.at[g], xr.at[g], sx.at[g], r_x.at[g], xn).wait_recv()
        total = pown[g] + dequantise(xr.at[g])

        @pl.when(t < ng - gz)
        def _():
            quantise(total, zs.at[g])
            slot = lax.rem(t, gz)
            remote(zs.at[g], zr.at[z, slot], sz.at[g], r_z.at[z, slot], (x, col, owner(t))).start()

        @pl.when(t >= ng - gz)
        def _():
            o_ref[lax.rem(t, gz)] += total

    def collect(t):
        src = lax.rem(z + nz - 1 - t // gz, nz)
        slot = lax.rem(t, gz)
        remote(zr.at[src, slot], zr.at[src, slot], sz.at[0], r_z.at[src, slot], xn).wait_recv()
        o_ref[slot] += dequantise(zr.at[src, slot])

    def step(t, carry):
        @pl.when(t < ng)
        def _():
            forward(t)

        @pl.when(jnp.logical_and(t >= 1, t < ng + 1))
        def _():
            onward(t - 1)

        @pl.when(t < ng - AHEAD)
        def _():
            begin(t + AHEAD)

        @pl.when(jnp.logical_and(t >= 2, t < ng + 2))
        def _():
            share(t - 2)

        @pl.when(t >= 3)
        def _():
            reduce(t - 3)

        @pl.when(t >= 3 + gz)
        def _():
            collect(t - 3 - gz)

        @pl.when(jnp.logical_and(t >= 2, t < ng + 2))
        def _():
            multiply(t - 2)

        return carry

    o_ref[...] = jnp.zeros_like(o_ref)
    lax.fori_loop(0, ng + 3, step, 0)

    def finish(t, carry):
        g = group(t)
        even = lax.rem(t, 2) == 0
        remote(st.at[g], st.at[g], s1.at[g], r_st.at[g], yn).wait_send()

        @pl.when(jnp.logical_or(home, jnp.logical_not(even)))
        def _():
            remote(st.at[g], st.at[g], s2.at[g], r_oth.at[g], xn).wait_send()

        remote(wv.at[g, :, crow, :], wv.at[g, :, crow, :], sc.at[g], r_c.at[g], sib).wait_send()
        remote(xs.at[g], xr.at[g], sx.at[g], r_x.at[g], xn).wait_send()

        @pl.when(t < ng - gz)
        def _():
            remote(zs.at[g], zs.at[g], sz.at[g], r_x.at[g], xn).wait_send()

        return carry

    lax.fori_loop(0, ng, finish, 0)


def fused(integrals, amplitudes, virt_count, occ_irrep):
    ng, ni, nk, cw, na = integrals.shape
    nj, nb = amplitudes.shape[1], amplitudes.shape[4]
    nz = lax.axis_size("rep")
    m, n, gz = ni * na, nj * nb, ng // nz
    dma = pltpu.SemaphoreType.DMA
    part = functools.partial
    coded = (m + PAD, n)
    return pl.pallas_call(
        part(kernel, nz),
        out_shape=jax.ShapeDtypeStruct((gz, m, n), jnp.float32),
        in_specs=[pl.BlockSpec(memory_space=pltpu.SMEM)] * 2 + [pl.BlockSpec(memory_space=pl.ANY)] * 2,
        out_specs=pl.BlockSpec(memory_space=pltpu.VMEM),
        scratch_shapes=[
            pltpu.VMEM((ng, nk, 2 * cw, 2 * m), jnp.bfloat16),
            pltpu.VMEM((nk, 2 * cw, 2 * m), jnp.bfloat16),
            pltpu.VMEM((ng, nk, 2 * cw, n), jnp.bfloat16),
            pltpu.VMEM((ng, nk, cw, m), jnp.bfloat16),
            pltpu.VMEM((ng, m, n), jnp.float32),
            pltpu.VMEM((ng,) + coded, jnp.int16),
            pltpu.VMEM((ng,) + coded, jnp.int16),
            pltpu.VMEM((ng,) + coded, jnp.int16),
            pltpu.VMEM((nz, gz) + coded, jnp.int16),
            dma((ng, nj)),
        ]
        + [dma((ng,))] * 11
        + [dma((nz, gz))],
        compiler_params=pltpu.CompilerParams(
            collective_id=0, has_side_effects=True, vmem_limit_bytes=56 * 1024 * 1024
        ),
    )(virt_count, occ_irrep, integrals, amplitudes)


def gathered(integrals, amplitudes, virt_count, occ_irrep):
    ngroup, _, k_local, c_local, nvirt = integrals.shape
    occ_local = lax.dynamic_slice_in_dim(occ_irrep, lax.axis_index("rep") * k_local, k_local)
    groups = jnp.arange(ngroup, dtype=jnp.int32)
    blocks = jnp.bitwise_xor(groups[:, None], occ_local[None, :])
    onehot = blocks[:, :, None] == groups[None, None, :]
    limit = jnp.sum(jnp.where(onehot, virt_count[None, None, :], 0), axis=2)
    c_global = lax.axis_index("col") * c_local + jnp.arange(c_local, dtype=jnp.int32)
    c_live = c_global[None, None, :] < limit[:, :, None]
    a_live = jnp.arange(nvirt, dtype=jnp.int32)[None, :] < virt_count[:, None]
    keep = c_live[:, None, :, :, None] & a_live[:, None, None, None, :]
    masked = jnp.where(keep, integrals, jnp.zeros_like(integrals))
    partial_cycle = contract(masked, amplitudes)
    return lax.psum_scatter(partial_cycle, "rep", scatter_dimension=0, tiled=True)


def body(integrals, amplitudes, virt_count, occ_irrep):
    ngroup, ni, _, c_local, nvirt = integrals.shape
    nj = amplitudes.shape[1]
    owned = ngroup // lax.axis_size("rep")
    if lax.axis_size("row") == 2 and lax.axis_size("col") == 4 and amplitudes.shape[3] == 2 * c_local:
        summed = fused(integrals, amplitudes, virt_count, occ_irrep)
        summed = summed.reshape(owned, ni, nvirt, nj, nvirt)
    else:
        summed = gathered(integrals, amplitudes, virt_count, occ_irrep)
    own_counts = lax.dynamic_slice_in_dim(virt_count, lax.axis_index("rep") * owned, owned)
    b_live = jnp.arange(nvirt, dtype=jnp.int32)[None, :] < own_counts[:, None]
    result = jnp.where(b_live[:, None, None, None, :], summed, jnp.zeros_like(summed))
    return result.astype(jnp.bfloat16)


def solution(mesh):
    return jax.shard_map(
        body,
        mesh=mesh,
        in_specs=(P(None, "row", "rep", "col", None), P(None, "col", "rep", "row", None), P(), P()),
        out_specs=P("rep", "row", None, "col", None),
        check_vma=False,
    )
```

```python
import functools

import jax
import jax.numpy as jnp
from jax import lax
from jax.experimental import pallas as pl
from jax.experimental.pallas import tpu as pltpu
from jax.sharding import PartitionSpec as P

MESH = pl.DeviceIdType.MESH
TOP = 32767.0
PAD = 16
AHEAD = 2
LAG = 4


def contract(w_part, t_part):
    w_full = lax.all_gather(w_part, "col", axis=3, tiled=True)
    return jnp.einsum(
        "gikca,gjkcb->giajb",
        w_full,
        lax.all_gather(t_part, "row", axis=3, tiled=True),
        preferred_element_type=jnp.float32,
    )


def quantise(value, ref):
    rows = value.shape[0]
    most = jnp.max(jnp.abs(value), axis=0, keepdims=True)
    code = jnp.ceil(8.0 * jnp.log2(jnp.maximum(most, 1e-30)))
    scaled = jnp.clip(jnp.round(value * (jnp.exp2(code * -0.125) * TOP)), -TOP, TOP)
    ref[0:rows, :] = scaled.astype(jnp.int32).astype(jnp.int16)
    wide = jnp.broadcast_to(code, (PAD, value.shape[1]))
    ref[rows : rows + PAD, :] = wide.astype(jnp.int32).astype(jnp.int16)


def dequantise(ref):
    rows = ref.shape[0] - PAD
    code = ref[rows : rows + PAD, :].astype(jnp.int32).astype(jnp.float32)[0:1, :]
    return ref[0:rows, :].astype(jnp.int32).astype(jnp.float32) * (jnp.exp2(code * 0.125) * (1.0 / TOP))


def kernel(nz, count_ref, occ_ref, w_ref, t_ref, o_ref, wv, wm, tv, st, pown, xs, xr, zs, zr,
           t_sem, l_sem, s1, s2, sc, sx, sz, r_own, r_oth, r_st, r_c, r_x, r_z):
    ng, ni, nk, cw, na = w_ref.shape
    m = ni * na
    nj, nb = t_ref.shape[1], t_ref.shape[4]
    n = nj * nb
    depth = nk * 2 * cw
    gz = ng // nz
    x, col, z = lax.axis_index("row"), lax.axis_index("col"), lax.axis_index("rep")
    y, core = col // 2, col % 2
    xn = (1 - x, col, z)
    yn = (x, (1 - y) * 2 + core, z)
    sib = (x, y * 2 + 1 - core, z)
    home = x == y
    away = x != y
    crow = pl.ds(pl.multiple_of(core * cw, cw), cw)
    crow_sib = pl.ds(pl.multiple_of((1 - core) * cw, cw), cw)
    own = pl.ds(pl.multiple_of(x * m, m), m)
    oth = pl.ds(pl.multiple_of((1 - x) * m, m), m)

    def group(t):
        return lax.rem(z + 1 + t // gz, nz) * gz + lax.rem(t, gz)

    def remote(src, dst, send, recv, dev):
        return pltpu.make_async_remote_copy(
            src_ref=src, dst_ref=dst, send_sem=send, recv_sem=recv, device_id=dev, device_id_type=MESH
        )

    def wait_oth(g):
        remote(wv.at[g, :, crow, oth], wv.at[g, :, crow, oth], s2.at[g], r_oth.at[g], xn).wait_recv()

    barrier = pltpu.get_barrier_semaphore()
    others = [xn, yn, sib] + [(x, col, lax.rem(z + d, nz)) for d in range(1, nz)]
    for dev in others:
        pl.semaphore_signal(barrier, inc=1, device_id=dev, device_id_type=MESH)
    pl.semaphore_wait(barrier, len(others))

    def pieces(g, dst, send, recv, dev):
        for i in range(ni):
            remote(w_ref.at[g, i], dst.at[:, :, pl.ds(i * na, na)], send, recv, dev).start()

    def begin(t):
        g = group(t)
        even = lax.rem(t, 2) == 0
        mine = wv.at[g, :, crow, own]

        @pl.when(home)
        def _():
            pieces(g, mine, s1.at[g], r_own.at[g], yn)
            for i in range(ni):
                pltpu.make_async_copy(w_ref.at[g, i], mine.at[:, :, pl.ds(i * na, na)], l_sem.at[g]).start()

        @pl.when(jnp.logical_and(away, even))
        def _():
            pieces(g, mine, s1.at[g], r_oth.at[g], xn)

        @pl.when(jnp.logical_and(away, jnp.logical_not(even)))
        def _():
            pieces(g, st.at[g], s1.at[g], r_st.at[g], yn)

        for j in range(nj):
            pltpu.make_async_copy(
                t_ref.at[g, j], tv.at[g, :, :, pl.ds(j * nb, nb)], t_sem.at[g, j]
            ).start()

    for t in range(AHEAD):
        begin(t)

    def forward(t):
        g = group(t)
        even = lax.rem(t, 2) == 0

        @pl.when(jnp.logical_and(home, jnp.logical_not(even)))
        def _():
            remote(st.at[g], st.at[g], s1.at[g], r_st.at[g], yn).wait_recv()
            remote(st.at[g], wv.at[g, :, crow, own], s2.at[g], r_oth.at[g], xn).start()

        @pl.when(jnp.logical_and(home, even))
        def _():
            wait_oth(g)
            remote(wv.at[g, :, crow, oth], wv.at[g, :, crow, oth], s2.at[g], r_oth.at[g], yn).start()

    def onward(t):
        g = group(t)

        @pl.when(jnp.logical_and(away, lax.rem(t, 2) == 1))
        def _():
            wait_oth(g)
            remote(wv.at[g, :, crow, oth], wv.at[g, :, crow, oth], s2.at[g], r_oth.at[g], yn).start()

    def share(t):
        g = group(t)
        even = lax.rem(t, 2) == 0

        @pl.when(home != even)
        def _():
            wait_oth(g)

        @pl.when(home)
        def _():
            pltpu.make_async_copy(st.at[g], wv.at[g, :, crow, own], l_sem.at[g]).wait()

        @pl.when(away)
        def _():
            remote(st.at[g], wv.at[g, :, crow, own], s1.at[g], r_own.at[g], yn).wait_recv()

        remote(wv.at[g, :, crow, :], wv.at[g, :, crow, :], sc.at[g], r_c.at[g], sib).start()

    def product(g, lanes):
        return lax.dot_general(
            wm[:, :, lanes].reshape(depth, m),
            tv[g].reshape(depth, n),
            (((0,), (0,)), ((), ())),
            preferred_element_type=jnp.float32,
        )

    def multiply(t):
        g = group(t)
        for j in range(nj):
            pltpu.make_async_copy(
                t_ref.at[g, j], tv.at[g, :, :, pl.ds(j * nb, nb)], t_sem.at[g, j]
            ).wait()
        remote(wv.at[g, :, crow, :], wv.at[g, :, crow_sib, :], sc.at[g], r_c.at[g], sib).wait_recv()
        rows = x * (2 * cw) + lax.broadcasted_iota(jnp.int32, (2 * cw, 2 * m), 0)
        a_live = lax.rem(lax.broadcasted_iota(jnp.int32, (2 * cw, 2 * m), 1), na) < count_ref[g]
        for k in range(nk):
            limit = count_ref[jnp.bitwise_xor(g, occ_ref[z * nk + k])]
            keep = jnp.where(jnp.logical_and(a_live, rows < limit), 1.0, 0.0).astype(jnp.bfloat16)
            wm[k] = wv[g, k] * keep
        quantise(product(g, oth), xs.at[g])
        remote(xs.at[g], xr.at[g], sx.at[g], r_x.at[g], xn).start()
        pown[g] = product(g, own)

    def owner(t):
        return lax.rem(z + 1 + t // gz, nz)

    def reduce(t):
        g = group(t)
        remote(xs.at[g], xr.at[g], sx.at[g], r_x.at[g], xn).wait_recv()
        total = pown[g] + dequantise(xr.at[g])

        @pl.when(t < ng - gz)
        def _():
            quantise(total, zs.at[g])
            slot = lax.rem(t, gz)
            remote(zs.at[g], zr.at[z, slot], sz.at[g], r_z.at[z, slot], (x, col, owner(t))).start()

        @pl.when(t >= ng - gz)
        def _():
            o_ref[lax.rem(t, gz)] += total

    def collect(t):
        src = lax.rem(z + nz - 1 - t // gz, nz)
        slot = lax.rem(t, gz)
        remote(zr.at[src, slot], zr.at[src, slot], sz.at[0], r_z.at[src, slot], xn).wait_recv()
        o_ref[slot] += dequantise(zr.at[src, slot])

    def step(t, carry):
        @pl.when(t < ng)
        def _():
            forward(t)

        @pl.when(jnp.logical_and(t >= 1, t < ng + 1))
        def _():
            onward(t - 1)

        @pl.when(t < ng - AHEAD)
        def _():
            begin(t + AHEAD)

        @pl.when(jnp.logical_and(t >= 2, t < ng + 2))
        def _():
            share(t - 2)

        @pl.when(t >= LAG + gz)
        def _():
            collect(t - LAG - gz)

        @pl.when(jnp.logical_and(t >= 2, t < ng + 2))
        def _():
            multiply(t - 2)

        @pl.when(t >= LAG)
        def _():
            reduce(t - LAG)

        return carry

    o_ref[...] = jnp.zeros_like(o_ref)
    lax.fori_loop(0, ng + LAG, step, 0)

    def finish(t, carry):
        g = group(t)
        even = lax.rem(t, 2) == 0
        remote(st.at[g], st.at[g], s1.at[g], r_st.at[g], yn).wait_send()

        @pl.when(jnp.logical_or(home, jnp.logical_not(even)))
        def _():
            remote(st.at[g], st.at[g], s2.at[g], r_oth.at[g], xn).wait_send()

        remote(wv.at[g, :, crow, :], wv.at[g, :, crow, :], sc.at[g], r_c.at[g], sib).wait_send()
        remote(xs.at[g], xr.at[g], sx.at[g], r_x.at[g], xn).wait_send()

        @pl.when(t < ng - gz)
        def _():
            remote(zs.at[g], zs.at[g], sz.at[g], r_x.at[g], xn).wait_send()

        return carry

    lax.fori_loop(0, ng, finish, 0)


def fused(integrals, amplitudes, virt_count, occ_irrep):
    ng, ni, nk, cw, na = integrals.shape
    nj, nb = amplitudes.shape[1], amplitudes.shape[4]
    nz = lax.axis_size("rep")
    m, n, gz = ni * na, nj * nb, ng // nz
    dma = pltpu.SemaphoreType.DMA
    part = functools.partial
    coded = (m + PAD, n)
    return pl.pallas_call(
        part(kernel, nz),
        out_shape=jax.ShapeDtypeStruct((gz, m, n), jnp.float32),
        in_specs=[pl.BlockSpec(memory_space=pltpu.SMEM)] * 2 + [pl.BlockSpec(memory_space=pl.ANY)] * 2,
        out_specs=pl.BlockSpec(memory_space=pltpu.VMEM),
        scratch_shapes=[
            pltpu.VMEM((ng, nk, 2 * cw, 2 * m), jnp.bfloat16),
            pltpu.VMEM((nk, 2 * cw, 2 * m), jnp.bfloat16),
            pltpu.VMEM((ng, nk, 2 * cw, n), jnp.bfloat16),
            pltpu.VMEM((ng, nk, cw, m), jnp.bfloat16),
            pltpu.VMEM((ng, m, n), jnp.float32),
            pltpu.VMEM((ng,) + coded, jnp.int16),
            pltpu.VMEM((ng,) + coded, jnp.int16),
            pltpu.VMEM((ng,) + coded, jnp.int16),
            pltpu.VMEM((nz, gz) + coded, jnp.int16),
            dma((ng, nj)),
        ]
        + [dma((ng,))] * 11
        + [dma((nz, gz))],
        compiler_params=pltpu.CompilerParams(
            collective_id=0, has_side_effects=True, vmem_limit_bytes=56 * 1024 * 1024
        ),
    )(virt_count, occ_irrep, integrals, amplitudes)


def gathered(integrals, amplitudes, virt_count, occ_irrep):
    ngroup, _, k_local, c_local, nvirt = integrals.shape
    occ_local = lax.dynamic_slice_in_dim(occ_irrep, lax.axis_index("rep") * k_local, k_local)
    groups = jnp.arange(ngroup, dtype=jnp.int32)
    blocks = jnp.bitwise_xor(groups[:, None], occ_local[None, :])
    onehot = blocks[:, :, None] == groups[None, None, :]
    limit = jnp.sum(jnp.where(onehot, virt_count[None, None, :], 0), axis=2)
    c_global = lax.axis_index("col") * c_local + jnp.arange(c_local, dtype=jnp.int32)
    c_live = c_global[None, None, :] < limit[:, :, None]
    a_live = jnp.arange(nvirt, dtype=jnp.int32)[None, :] < virt_count[:, None]
    keep = c_live[:, None, :, :, None] & a_live[:, None, None, None, :]
    masked = jnp.where(keep, integrals, jnp.zeros_like(integrals))
    partial_cycle = contract(masked, amplitudes)
    return lax.psum_scatter(partial_cycle, "rep", scatter_dimension=0, tiled=True)


def body(integrals, amplitudes, virt_count, occ_irrep):
    ngroup, ni, _, c_local, nvirt = integrals.shape
    nj = amplitudes.shape[1]
    owned = ngroup // lax.axis_size("rep")
    if lax.axis_size("row") == 2 and lax.axis_size("col") == 4 and amplitudes.shape[3] == 2 * c_local:
        summed = fused(integrals, amplitudes, virt_count, occ_irrep)
        summed = summed.reshape(owned, ni, nvirt, nj, nvirt)
    else:
        summed = gathered(integrals, amplitudes, virt_count, occ_irrep)
    own_counts = lax.dynamic_slice_in_dim(virt_count, lax.axis_index("rep") * owned, owned)
    b_live = jnp.arange(nvirt, dtype=jnp.int32)[None, :] < own_counts[:, None]
    result = jnp.where(b_live[:, None, None, None, :], summed, jnp.zeros_like(summed))
    return result.astype(jnp.bfloat16)


def solution(mesh):
    return jax.shard_map(
        body,
        mesh=mesh,
        in_specs=(P(None, "row", "rep", "col", None), P(None, "col", "rep", "row", None), P(), P()),
        out_specs=P("rep", "row", None, "col", None),
        check_vma=False,
    )
```

```python
import functools

import jax
import jax.numpy as jnp
from jax import lax
from jax.experimental import pallas as pl
from jax.experimental.pallas import tpu as pltpu
from jax.sharding import PartitionSpec as P

MESH = pl.DeviceIdType.MESH
TOP = 32767.0
PAD = 16
AHEAD = 2
LAG = 3
SLACK = 4


def contract(w_part, t_part):
    w_full = lax.all_gather(w_part, "col", axis=3, tiled=True)
    return jnp.einsum(
        "gikca,gjkcb->giajb",
        w_full,
        lax.all_gather(t_part, "row", axis=3, tiled=True),
        preferred_element_type=jnp.float32,
    )


def quantise(value, ref):
    rows = value.shape[0]
    most = jnp.max(jnp.abs(value), axis=0, keepdims=True)
    code = jnp.ceil(8.0 * jnp.log2(jnp.maximum(most, 1e-30)))
    scaled = jnp.clip(jnp.round(value * (jnp.exp2(code * -0.125) * TOP)), -TOP, TOP)
    ref[0:rows, :] = scaled.astype(jnp.int32).astype(jnp.int16)
    wide = jnp.broadcast_to(code, (PAD, value.shape[1]))
    ref[rows : rows + PAD, :] = wide.astype(jnp.int32).astype(jnp.int16)


def dequantise(ref):
    rows = ref.shape[0] - PAD
    code = ref[rows : rows + PAD, :].astype(jnp.int32).astype(jnp.float32)[0:1, :]
    return ref[0:rows, :].astype(jnp.int32).astype(jnp.float32) * (jnp.exp2(code * 0.125) * (1.0 / TOP))


def kernel(nz, count_ref, occ_ref, w_ref, t_ref, o_ref, wv, wm, tv, st, pown, xs, xr, zs, zr,
           t_sem, l_sem, s1, s2, sc, sx, sz, r_own, r_oth, r_st, r_c, r_x, r_z):
    ng, ni, nk, cw, na = w_ref.shape
    m = ni * na
    nj, nb = t_ref.shape[1], t_ref.shape[4]
    n = nj * nb
    depth = nk * 2 * cw
    gz = ng // nz
    x, col, z = lax.axis_index("row"), lax.axis_index("col"), lax.axis_index("rep")
    y, core = col // 2, col % 2
    xn = (1 - x, col, z)
    yn = (x, (1 - y) * 2 + core, z)
    sib = (x, y * 2 + 1 - core, z)
    home = x == y
    away = x != y
    crow = pl.ds(pl.multiple_of(core * cw, cw), cw)
    crow_sib = pl.ds(pl.multiple_of((1 - core) * cw, cw), cw)
    own = pl.ds(pl.multiple_of(x * m, m), m)
    oth = pl.ds(pl.multiple_of((1 - x) * m, m), m)

    def group(t):
        return lax.rem(z + 1 + t // gz, nz) * gz + lax.rem(t, gz)

    def remote(src, dst, send, recv, dev):
        return pltpu.make_async_remote_copy(
            src_ref=src, dst_ref=dst, send_sem=send, recv_sem=recv, device_id=dev, device_id_type=MESH
        )

    def wait_oth(g):
        remote(wv.at[g, :, crow, oth], wv.at[g, :, crow, oth], s2.at[g], r_oth.at[g], xn).wait_recv()

    barrier = pltpu.get_barrier_semaphore()
    others = [xn, yn, sib] + [(x, col, lax.rem(z + d, nz)) for d in range(1, nz)]
    for dev in others:
        pl.semaphore_signal(barrier, inc=1, device_id=dev, device_id_type=MESH)
    pl.semaphore_wait(barrier, len(others))

    def pieces(g, dst, send, recv, dev):
        for i in range(ni):
            remote(w_ref.at[g, i], dst.at[:, :, pl.ds(i * na, na)], send, recv, dev).start()

    def begin(t):
        g = group(t)
        even = lax.rem(t, 2) == 0
        mine = wv.at[g, :, crow, own]

        @pl.when(home)
        def _():
            pieces(g, mine, s1.at[g], r_own.at[g], yn)
            for i in range(ni):
                pltpu.make_async_copy(w_ref.at[g, i], mine.at[:, :, pl.ds(i * na, na)], l_sem.at[g]).start()

        @pl.when(jnp.logical_and(away, even))
        def _():
            pieces(g, mine, s1.at[g], r_oth.at[g], xn)

        @pl.when(jnp.logical_and(away, jnp.logical_not(even)))
        def _():
            pieces(g, st.at[g], s1.at[g], r_st.at[g], yn)

        for j in range(nj):
            pltpu.make_async_copy(
                t_ref.at[g, j], tv.at[g, :, :, pl.ds(j * nb, nb)], t_sem.at[g, j]
            ).start()

    for t in range(AHEAD):
        begin(t)

    def forward(t):
        g = group(t)
        even = lax.rem(t, 2) == 0

        @pl.when(jnp.logical_and(home, jnp.logical_not(even)))
        def _():
            remote(st.at[g], st.at[g], s1.at[g], r_st.at[g], yn).wait_recv()
            remote(st.at[g], wv.at[g, :, crow, own], s2.at[g], r_oth.at[g], xn).start()

        @pl.when(jnp.logical_and(home, even))
        def _():
            wait_oth(g)
            remote(wv.at[g, :, crow, oth], wv.at[g, :, crow, oth], s2.at[g], r_oth.at[g], yn).start()

    def onward(t):
        g = group(t)

        @pl.when(jnp.logical_and(away, lax.rem(t, 2) == 1))
        def _():
            wait_oth(g)
            remote(wv.at[g, :, crow, oth], wv.at[g, :, crow, oth], s2.at[g], r_oth.at[g], yn).start()

    def share(t):
        g = group(t)
        even = lax.rem(t, 2) == 0

        @pl.when(home != even)
        def _():
            wait_oth(g)

        @pl.when(home)
        def _():
            pltpu.make_async_copy(st.at[g], wv.at[g, :, crow, own], l_sem.at[g]).wait()

        @pl.when(away)
        def _():
            remote(st.at[g], wv.at[g, :, crow, own], s1.at[g], r_own.at[g], yn).wait_recv()

        remote(wv.at[g, :, crow, :], wv.at[g, :, crow, :], sc.at[g], r_c.at[g], sib).start()

    def product(g, lanes):
        return lax.dot_general(
            wm[:, :, lanes].reshape(depth, m),
            tv[g].reshape(depth, n),
            (((0,), (0,)), ((), ())),
            preferred_element_type=jnp.float32,
        )

    def multiply(t):
        g = group(t)
        for j in range(nj):
            pltpu.make_async_copy(
                t_ref.at[g, j], tv.at[g, :, :, pl.ds(j * nb, nb)], t_sem.at[g, j]
            ).wait()
        remote(wv.at[g, :, crow, :], wv.at[g, :, crow_sib, :], sc.at[g], r_c.at[g], sib).wait_recv()
        rows = x * (2 * cw) + lax.broadcasted_iota(jnp.int32, (2 * cw, 2 * m), 0)
        a_live = lax.rem(lax.broadcasted_iota(jnp.int32, (2 * cw, 2 * m), 1), na) < count_ref[g]
        for k in range(nk):
            limit = count_ref[jnp.bitwise_xor(g, occ_ref[z * nk + k])]
            keep = jnp.where(jnp.logical_and(a_live, rows < limit), 1.0, 0.0).astype(jnp.bfloat16)
            wm[k] = wv[g, k] * keep
        quantise(product(g, oth), xs.at[g])
        remote(xs.at[g], xr.at[g], sx.at[g], r_x.at[g], xn).start()
        pown[g] = product(g, own)

    def owner(t):
        return lax.rem(z + 1 + t // gz, nz)

    def reduce(t):
        g = group(t)
        remote(xs.at[g], xr.at[g], sx.at[g], r_x.at[g], xn).wait_recv()
        total = pown[g] + dequantise(xr.at[g])

        @pl.when(t < ng - gz)
        def _():
            quantise(total, zs.at[g])
            slot = lax.rem(t, gz)
            remote(zs.at[g], zr.at[z, slot], sz.at[g], r_z.at[z, slot], (x, col, owner(t))).start()

        @pl.when(t >= ng - gz)
        def _():
            o_ref[lax.rem(t, gz)] += total

    def collect(t):
        src = lax.rem(z + nz - 1 - t // gz, nz)
        slot = lax.rem(t, gz)
        remote(zr.at[src, slot], zr.at[src, slot], sz.at[0], r_z.at[src, slot], xn).wait_recv()
        o_ref[slot] += dequantise(zr.at[src, slot])

    def step(t, carry):
        @pl.when(t < ng)
        def _():
            forward(t)

        @pl.when(jnp.logical_and(t >= 1, t < ng + 1))
        def _():
            onward(t - 1)

        @pl.when(t < ng - AHEAD)
        def _():
            begin(t + AHEAD)

        @pl.when(jnp.logical_and(t >= 2, t < ng + 2))
        def _():
            share(t - 2)

        @pl.when(jnp.logical_and(t >= 2, t < ng + 2))
        def _():
            multiply(t - 2)

        @pl.when(t >= LAG)
        def _():
            reduce(t - LAG)

        @pl.when(t >= LAG + SLACK)
        def _():
            collect(t - LAG - SLACK)

        return carry

    o_ref[...] = jnp.zeros_like(o_ref)
    lax.fori_loop(0, ng + LAG, step, 0)

    def rest(t, carry):
        collect(t)
        return carry

    lax.fori_loop(ng - SLACK, ng - gz, rest, 0)

    def finish(t, carry):
        g = group(t)
        even = lax.rem(t, 2) == 0
        remote(st.at[g], st.at[g], s1.at[g], r_st.at[g], yn).wait_send()

        @pl.when(jnp.logical_or(home, jnp.logical_not(even)))
        def _():
            remote(st.at[g], st.at[g], s2.at[g], r_oth.at[g], xn).wait_send()

        remote(wv.at[g, :, crow, :], wv.at[g, :, crow, :], sc.at[g], r_c.at[g], sib).wait_send()
        remote(xs.at[g], xr.at[g], sx.at[g], r_x.at[g], xn).wait_send()

        @pl.when(t < ng - gz)
        def _():
            remote(zs.at[g], zs.at[g], sz.at[g], r_x.at[g], xn).wait_send()

        return carry

    lax.fori_loop(0, ng, finish, 0)


def fused(integrals, amplitudes, virt_count, occ_irrep):
    ng, ni, nk, cw, na = integrals.shape
    nj, nb = amplitudes.shape[1], amplitudes.shape[4]
    nz = lax.axis_size("rep")
    m, n, gz = ni * na, nj * nb, ng // nz
    dma = pltpu.SemaphoreType.DMA
    part = functools.partial
    coded = (m + PAD, n)
    return pl.pallas_call(
        part(kernel, nz),
        out_shape=jax.ShapeDtypeStruct((gz, m, n), jnp.float32),
        in_specs=[pl.BlockSpec(memory_space=pltpu.SMEM)] * 2 + [pl.BlockSpec(memory_space=pl.ANY)] * 2,
        out_specs=pl.BlockSpec(memory_space=pltpu.VMEM),
        scratch_shapes=[
            pltpu.VMEM((ng, nk, 2 * cw, 2 * m), jnp.bfloat16),
            pltpu.VMEM((nk, 2 * cw, 2 * m), jnp.bfloat16),
            pltpu.VMEM((ng, nk, 2 * cw, n), jnp.bfloat16),
            pltpu.VMEM((ng, nk, cw, m), jnp.bfloat16),
            pltpu.VMEM((ng, m, n), jnp.float32),
            pltpu.VMEM((ng,) + coded, jnp.int16),
            pltpu.VMEM((ng,) + coded, jnp.int16),
            pltpu.VMEM((ng,) + coded, jnp.int16),
            pltpu.VMEM((nz, gz) + coded, jnp.int16),
            dma((ng, nj)),
        ]
        + [dma((ng,))] * 11
        + [dma((nz, gz))],
        compiler_params=pltpu.CompilerParams(
            collective_id=0, has_side_effects=True, vmem_limit_bytes=56 * 1024 * 1024
        ),
    )(virt_count, occ_irrep, integrals, amplitudes)


def gathered(integrals, amplitudes, virt_count, occ_irrep):
    ngroup, _, k_local, c_local, nvirt = integrals.shape
    occ_local = lax.dynamic_slice_in_dim(occ_irrep, lax.axis_index("rep") * k_local, k_local)
    groups = jnp.arange(ngroup, dtype=jnp.int32)
    blocks = jnp.bitwise_xor(groups[:, None], occ_local[None, :])
    onehot = blocks[:, :, None] == groups[None, None, :]
    limit = jnp.sum(jnp.where(onehot, virt_count[None, None, :], 0), axis=2)
    c_global = lax.axis_index("col") * c_local + jnp.arange(c_local, dtype=jnp.int32)
    c_live = c_global[None, None, :] < limit[:, :, None]
    a_live = jnp.arange(nvirt, dtype=jnp.int32)[None, :] < virt_count[:, None]
    keep = c_live[:, None, :, :, None] & a_live[:, None, None, None, :]
    masked = jnp.where(keep, integrals, jnp.zeros_like(integrals))
    partial_cycle = contract(masked, amplitudes)
    return lax.psum_scatter(partial_cycle, "rep", scatter_dimension=0, tiled=True)


def body(integrals, amplitudes, virt_count, occ_irrep):
    ngroup, ni, _, c_local, nvirt = integrals.shape
    nj = amplitudes.shape[1]
    owned = ngroup // lax.axis_size("rep")
    if lax.axis_size("row") == 2 and lax.axis_size("col") == 4 and amplitudes.shape[3] == 2 * c_local:
        summed = fused(integrals, amplitudes, virt_count, occ_irrep)
        summed = summed.reshape(owned, ni, nvirt, nj, nvirt)
    else:
        summed = gathered(integrals, amplitudes, virt_count, occ_irrep)
    own_counts = lax.dynamic_slice_in_dim(virt_count, lax.axis_index("rep") * owned, owned)
    b_live = jnp.arange(nvirt, dtype=jnp.int32)[None, :] < own_counts[:, None]
    result = jnp.where(b_live[:, None, None, None, :], summed, jnp.zeros_like(summed))
    return result.astype(jnp.bfloat16)


def solution(mesh):
    return jax.shard_map(
        body,
        mesh=mesh,
        in_specs=(P(None, "row", "rep", "col", None), P(None, "col", "rep", "row", None), P(), P()),
        out_specs=P("rep", "row", None, "col", None),
        check_vma=False,
    )
```
